32 devices in a mesh: dom: 8 (over z, core), col: 4 (over y, x).
Axes of the slice: x: 2, y: 2, z: 4, core: 2. Of those that a mesh axis runs over, the one named last changes fastest.
Arguments:
- features: bfloat16 [768, 32768], P('col', 'dom'), may hold values from -6 to 6
- tiles: bfloat16 [512, 128, 128], P('dom'), may hold values from -0.3984375 to 0.3984375
- tile_src_part: int32 [512, 1], P('dom'), may hold values from 0 to 7; in each aligned block of 64 rows (0 to 63, 64 to 127, ...) at most 16 rows name the same one
- tile_src_block: int32 [512], P('dom'), may hold values from 0 to 31
- tile_dst_block: int32 [512], P('dom'), may hold values from 0 to 23
- tile_count: int32 [8], P('dom'), may hold values from 1 to 64, 256 in all
- prior_hops: bfloat16 [2, 768, 24576], P(None, 'col', 'dom'), may hold values from -6 to 6
- labels: int32 [24576], P('dom'), may hold values from 0 to 152
- batch_of: int32 [24576, 1], P('dom'), may hold values from 0 to 15; in each aligned block of 3072 rows (0 to 3071, 3072 to 6143, ...) at most 240 rows name the same one
- w1: bfloat16 [4, 768, 1024], P(None, 'col'), may hold values from -0.109375 to 0.109375
- w2: bfloat16 [1024, 153], P('col')
Outputs:
- propagated: bfloat16 [768, 24576], P('col', 'dom')
- w1_new: float32 [4, 768, 1024], P(None, 'col')
- w2_new: float32 [1024, 153], P('col')
The draws below stay inside these ranges and needn't reach their ends.
Inputs may be any that keep to these rules, and one draw needn't show every extreme that they name: `tile_src_part`: in the tile slots of one part no source part is named more than 16 times. `batch_of`: among the destination rows of one part no minibatch is named more than 240 times.
All inputs are finite; a program needn't handle non-finite values. No bound on the sum of `tile_count` on one device may be relied on, other than what follows from the above.
Results may differ from the reference program's by a relative error of at most 0.025.
Values may be sent and summed in bfloat16 or wider, within the bound.
A program may use at most 128 MiB of HBM per device.

```python
import math
import jax
import jax.numpy as jnp
import numpy as np
from jax import lax

D = 768
HID = 1024
CLASSES = 153
HOPS = 4
BLK = 128
STEPS = 2
SBLK = 32
DBLK = 24
TILE_CAP = 64
TCAP = 16
DROWS = 3072
CAPM = 240
SOURCES = 32768
DESTS = 24576
TILES = 512
N_DOM = 8
N_COL = 4


def draw_w2(key, part):
    key = jax.random.fold_in(key, 11)
    base = jax.random.normal(key, (HID, CLASSES), jnp.float32) / math.sqrt(HID)
    return base.astype(jnp.bfloat16)


def place_ends(entries, key, least, high):
    shape = entries.shape
    index_at = [jax.random.randint(jax.random.fold_in(key, axis), (), 0, shape[axis]) for axis in range(len(shape))]
    entries = entries.at[tuple(index_at)].set(least)
    longest = shape.index(max(shape))
    index_at[longest] = (index_at[longest] + 1) % shape[longest]
    return entries.at[tuple(index_at)].set(high)


def shard_levels(stream_key, dims, split, least, largest):
    def one(dim, blocks):
        draws = jax.random.uniform(jax.random.fold_in(jax.random.fold_in(stream_key, 6), dim), (blocks,), jnp.float32, least / len(split), largest / len(split))
        return jnp.repeat(jnp.exp(draws), dims[dim] // blocks).reshape((-1,) + (1,) * (len(dims) - dim - 1))

    loudness = one(*split[0])
    for cut in split[1:]:
        loudness = loudness * one(*cut)
    return loudness


def split_up(amount, total, bound, lean):
    loads = [(1 << 20) // math.isqrt(rank ** lean) + 1 for rank in range(2, amount + 1)]
    spare, holding = total - bound - (amount - 1), [1] * (amount - 1)
    while spare > 0:
        movable = [i for i in range(amount - 1) if holding[i] < bound]
        pool, remaining = sum([loads[i] for i in movable]), spare
        for i in movable:
            extra = min(bound - holding[i], max(1, remaining * loads[i] // pool), spare)
            holding[i] = holding[i] + extra
            spare = spare - extra
    return np.array([bound] + holding)


def uneven_parts(rng, count, total, limit, lean):
    if count == 2:
        one = jax.random.randint(rng, (), max(1, total - limit), min(limit, total - 1) + 1)
        return jnp.stack([one, total - one])
    lengths = jnp.asarray(split_up(count, total, limit, lean), jnp.int32)
    couples = (count - 1) // 2
    giver, receiver = lengths[1:1 + 2 * couples:2], lengths[2:2 + 2 * couples:2]
    room = jnp.minimum(giver - 1, limit - receiver)
    passed = jax.random.randint(jax.random.fold_in(rng, 1), (couples,), 0, 1 << 20) % (room + 1)
    lengths = lengths.at[1:1 + 2 * couples:2].set(giver - passed).at[2:2 + 2 * couples:2].set(receiver + passed)
    return lengths[jax.random.permutation(jax.random.fold_in(rng, 2), count)]


def assign_block(rng, own, number, rows, amount, top, most, skew):
    order = jax.random.permutation(rng, amount)
    crowded, common = portions_of(amount, rows * top, most, skew, True), portions_of(amount, rows * top, most, skew, False)
    places = jnp.arange(amount)

    def named(tallies, rotation):
        used = int((tallies > 0).sum())
        fixed = max(1, used // 4)
        moved = fixed + (places - fixed + rotation * (used - fixed)) % max(1, amount - fixed)
        return jnp.zeros((amount,), jnp.int32).at[order[jnp.where(places < fixed, places, moved)]].set(jnp.asarray(tallies, jnp.int32))

    tallies = jnp.where(number % 4 == 0, named(crowded, number // 4), named(common, number - number // 4 - 1))
    mixed = jax.random.permutation(jax.random.fold_in(own, 3), amount)
    donor, sink = mixed[0:amount // 2 * 2:2], mixed[1:amount // 2 * 2:2]
    margin = jnp.minimum(tallies[donor] - 1, most - tallies[sink]) // 2
    margin = jnp.where((donor == order[0]) | (sink == order[0]) | (tallies[sink] == 0), 0, jnp.maximum(margin, 0))
    moved = jax.random.randint(jax.random.fold_in(own, 4), (amount // 2,), 0, 1 << 20) % (margin + 1)
    tallies = tallies.at[donor].add(-moved).at[sink].add(moved)
    items = jnp.searchsorted(jnp.cumsum(tallies), jnp.arange(rows * top), side="right").astype(jnp.int32)
    listing = items.reshape(top, rows).T
    listing = listing[jax.random.permutation(jax.random.fold_in(own, 1), rows)]
    rotation = jax.random.randint(jax.random.fold_in(own, 2), (rows, 1), 0, top)
    return jnp.take_along_axis(listing, (jnp.arange(top)[None, :] + rotation) % top, axis=1)


def portions_of(number_of, total, reach, lean, full):
    loads = [(1 << 20) // math.isqrt(standing ** lean) + 1 for standing in range(1, number_of + 1)]
    largest = reach if full else min(reach, max(-(-total // number_of), total * loads[0] // sum(loads)))
    least = 1 if total - largest >= number_of - 1 else 0
    counts, rest = [largest] + [least] * (number_of - 1), total - largest - least * (number_of - 1)
    while rest > 0:
        movable = [i for i in range(1, number_of) if counts[i] < largest] or [i for i in range(1, number_of) if counts[i] < reach]
        pool, budget = sum([loads[i] for i in movable]), rest
        for i in movable:
            extra = min(reach - counts[i], max(1, budget * loads[i] // pool), rest)
            counts[i] = counts[i] + extra
            rest = rest - extra
    return np.array(counts)


def noise(own_key, dims, deviation, most, cuts=(), held_as=jnp.bfloat16):
    loudness = shard_levels(own_key, dims, cuts, -0.22, 0.18) if cuts else 1.0
    values = jax.random.normal(own_key, dims, jnp.float32) * deviation * loudness
    return jnp.minimum(jnp.maximum(values, -most), most).astype(held_as)


def setup_inputs(seed: int = 0) -> dict:
    streams_of = jax.random.split(jax.random.key(seed), 12)
    features = noise(streams_of[0], (D, SOURCES), 1.0, 6.0, ((0, 4), (1, 8)))
    tiles = noise(streams_of[1], (TILES, BLK, BLK), 0.06, 0.3984375, ((0, 8),))
    tile_src_part_keys = jax.random.split(jax.random.fold_in(streams_of[2], 1), TILES // TILE_CAP)
    tile_src_part_turns = jax.random.permutation(jax.random.fold_in(streams_of[2], 3), TILES // TILE_CAP)
    tile_src_part = jax.vmap(lambda own, number: assign_block(jax.random.fold_in(streams_of[2], 2), own, number, TILE_CAP, N_DOM, 1, TCAP, 2))(tile_src_part_keys, tile_src_part_turns).reshape((TILES, 1))
    tile_src_block = place_ends(jax.random.randint(streams_of[3], (TILES,), 0, SBLK), jax.random.fold_in(streams_of[3], 1), 0, SBLK - 1).astype(jnp.int32)
    tile_dst_block = place_ends(jax.random.randint(streams_of[4], (TILES,), 0, DBLK), jax.random.fold_in(streams_of[4], 1), 0, DBLK - 1).astype(jnp.int32)
    tile_count = uneven_parts(streams_of[5], N_DOM, TILE_CAP * N_DOM // 2, TILE_CAP, 2).astype(jnp.int32)
    prior_hops = noise(streams_of[6], (2, D, DESTS), 1.0, 6.0, ((1, 4), (2, 8)))
    labels = place_ends(jax.random.randint(streams_of[7], (DESTS,), 0, CLASSES), jax.random.fold_in(streams_of[7], 1), 0, CLASSES - 1).astype(jnp.int32)
    batch_of_keys = jax.random.split(jax.random.fold_in(streams_of[8], 1), DESTS // DROWS)
    batch_of_turns = jax.random.permutation(jax.random.fold_in(streams_of[8], 3), DESTS // DROWS)
    batch_of = jax.vmap(lambda own, number: assign_block(jax.random.fold_in(streams_of[8], 2), own, number, DROWS, STEPS * N_DOM, 1, CAPM, 0))(batch_of_keys, batch_of_turns).reshape((DESTS, 1))
    w1 = noise(streams_of[9], (HOPS, D, HID), (HOPS * D) ** -0.5, 0.109375, ((1, 4),))
    w2 = draw_w2(jax.random.fold_in(streams_of[11], 71), 0)
    return dict(features=features, tiles=tiles, tile_src_part=tile_src_part, tile_src_block=tile_src_block, tile_dst_block=tile_dst_block, tile_count=tile_count, prior_hops=prior_hops, labels=labels, batch_of=batch_of, w1=w1, w2=w2)


step_rate = 0.02


def reference(features, tiles, tile_src_part, tile_src_block, tile_dst_block, tile_count, prior_hops, labels, batch_of, w1, w2):
    width = D // N_COL
    blocks = features.reshape(D, N_DOM * SBLK, BLK)
    gblock = (tile_src_part[:, 0] * SBLK + tile_src_block).astype(jnp.int32)
    slots = jnp.arange(TILES, dtype=jnp.int32) % TILE_CAP
    owners = jnp.arange(TILES, dtype=jnp.int32) // TILE_CAP
    valid = (slots < tile_count[owners]).astype(jnp.float32)

    def one_part(p):
        start = (p * TILE_CAP).astype(jnp.int32)
        picks = lax.dynamic_slice_in_dim(gblock, start, TILE_CAP)
        local = lax.dynamic_slice_in_dim(tiles, start, TILE_CAP).astype(jnp.float32)
        where_to = lax.dynamic_slice_in_dim(tile_dst_block, start, TILE_CAP)
        used = lax.dynamic_slice_in_dim(valid, start, TILE_CAP)
        source = jnp.take(blocks, picks, axis=1).astype(jnp.float32)
        contrib = jnp.einsum('dtk,tik->dti', source, local) * used[None, :, None]
        target = (where_to[:, None] == jnp.arange(DBLK, dtype=jnp.int32)[None, :]).astype(jnp.float32)
        return jnp.einsum('dti,tb->dbi', contrib, target).reshape(D, DROWS)

    stacked = lax.map(one_part, jnp.arange(N_DOM, dtype=jnp.int32))
    propagated = jnp.transpose(stacked, (1, 0, 2)).reshape(D, DESTS).astype(jnp.bfloat16)
    own = features.reshape(D, N_DOM, SBLK * BLK)[:, :, :DROWS].reshape(D, DESTS)
    inputs = jnp.stack([own, propagated, prior_hops[0], prior_hops[1]])
    sliced = inputs.reshape(HOPS, N_COL, width, DESTS)
    stepid = batch_of[:, 0] // N_DOM
    w1_master = w1.astype(jnp.float32)
    w2_master = w2.astype(jnp.float32)
    onehot = (labels[:, None] == jnp.arange(CLASSES, dtype=jnp.int32)[None, :]).astype(jnp.float32)
    for step in range(STEPS):
        member = (stepid == step).astype(jnp.float32)
        w1_low = w1_master.astype(jnp.bfloat16)
        w2_low = w2_master.astype(jnp.bfloat16)
        w1_sliced = w1_low.reshape(HOPS, N_COL, width, HID)

        def add_slice(index, total):
            xin = lax.dynamic_index_in_dim(sliced, index, 1, keepdims=False).astype(jnp.float32)
            wpart = lax.dynamic_index_in_dim(w1_sliced, index, 1, keepdims=False).astype(jnp.float32)
            partial_value = jnp.einsum('hdr,hdj->rj', xin, wpart)
            rounded = lax.optimization_barrier(partial_value.astype(jnp.bfloat16))
            return total + rounded.astype(jnp.float32)

        zsum = lax.fori_loop(0, N_COL, add_slice, jnp.zeros((DESTS, HID), jnp.float32))
        hidden = jax.nn.silu(zsum).astype(jnp.bfloat16)
        logits = jnp.dot(hidden, w2_low, preferred_element_type=jnp.float32)
        prob = jax.nn.softmax(logits, axis=-1)
        slope = ((prob - onehot) * member[:, None]).astype(jnp.bfloat16)
        grad2 = jnp.dot(hidden.T, slope, preferred_element_type=jnp.float32)
        back = jnp.dot(slope, w2_low.T, preferred_element_type=jnp.float32)
        sig = jax.nn.sigmoid(zsum)
        dz = (back * sig * (1.0 + zsum * (1.0 - sig))).astype(jnp.bfloat16)
        grad1 = jnp.einsum('hdr,rj->hdj', inputs.astype(jnp.float32), dz.astype(jnp.float32))
        w1_master = w1_master - step_rate * grad1
        w2_master = w2_master - step_rate * grad2
    return propagated, w1_master, w2_master
```

```python
import jax
import jax.numpy as jnp
from jax import lax
from jax.sharding import PartitionSpec as P

STEPS = 2


step_rate = 0.02


def per_device(
    features,
    tiles,
    tile_src_part,
    tile_src_block,
    tile_dst_block,
    tile_count,
    prior_hops,
    labels,
    batch_of,
    w1,
    w2,
):
    ndom = lax.axis_size("dom")
    ncol = lax.axis_size("col")
    col = lax.axis_index("col")
    width, srows = features.shape
    tilecap, blk, _unused = tiles.shape
    sblk = srows // blk
    drows = prior_hops.shape[2]
    dblk = drows // blk
    hops = w1.shape[0]
    classes = w2.shape[1]
    hid = w1.shape[2]

    buckets = STEPS * ndom
    capm = (5 * drows + 4 * buckets - 1) // (4 * buckets)
    window = min(drows, ndom * capm)
    step_of = batch_of[:, 0] // ndom
    first = (step_of == 0).astype(jnp.int32)
    rank = jnp.cumsum(first)
    n_first = rank[drows - 1]
    index = jnp.arange(drows, dtype=jnp.int32)
    place = jnp.where(first == 1, rank - 1, n_first + index - rank)
    moves = (place[:, None] == index[None, :]).astype(jnp.bfloat16)

    blocks = features.reshape(width, sblk, blk)
    piece = lax.all_gather(blocks, "dom", axis=1, tiled=True)
    w2_master = lax.all_gather(w2, "col", axis=0, tiled=True).astype(jnp.float32)

    known = jnp.concatenate(
        [features[:, :drows], prior_hops[0], prior_hops[1]], axis=0
    )
    known = jnp.dot(known, moves, preferred_element_type=jnp.float32).astype(jnp.bfloat16)
    tags = jnp.dot(
        jnp.broadcast_to(labels.astype(jnp.bfloat16)[None, :], (8, drows)),
        moves,
        preferred_element_type=jnp.float32,
    )[0].astype(jnp.int32)

    valid = (jnp.arange(tilecap, dtype=jnp.int32) < tile_count[0]).astype(jnp.float32)
    gblock = tile_src_part[:, 0] * sblk + tile_src_block
    sources = jnp.take(piece, gblock, axis=1, mode="clip")
    contrib = (
        jnp.einsum("dtk,tik->dti", sources, tiles, preferred_element_type=jnp.float32)
        * valid[None, :, None]
    )
    target = (tile_dst_block[:, None] == jnp.arange(dblk, dtype=jnp.int32)[None, :]).astype(
        jnp.float32
    )
    summed = jnp.einsum("dti,tb->dbi", contrib, target, precision=lax.Precision.HIGHEST)
    propagated = summed.reshape(width, drows).astype(jnp.bfloat16)
    fresh = jnp.dot(propagated, moves, preferred_element_type=jnp.float32).astype(jnp.bfloat16)
    flat = jnp.concatenate([known[:width], fresh, known[width:]], axis=0)

    share = window // ncol
    w1_master = w1.reshape(hops * width, hid).astype(jnp.float32)
    for step in range(STEPS):
        start = 0 if step == 0 else drows - window
        batch_x = lax.slice_in_dim(flat, start, start + window, axis=1)
        spot = start + col * share + jnp.arange(share, dtype=jnp.int32)
        batch_label = lax.dynamic_slice_in_dim(tags, start + col * share, share)
        member = (spot < n_first) if step == 0 else (spot >= n_first)
        member = member.astype(jnp.float32)
        w1_low = w1_master.astype(jnp.bfloat16)
        w2_low = w2_master.astype(jnp.bfloat16)
        partial_value = jnp.einsum(
            "dr,dj->rj", batch_x, w1_low, preferred_element_type=jnp.float32
        ).astype(jnp.bfloat16)
        z = lax.psum_scatter(
            partial_value, "col", scatter_dimension=0, tiled=True
        ).astype(jnp.float32)
        hidden = jax.nn.silu(z).astype(jnp.bfloat16)
        logits = jnp.dot(hidden, w2_low, preferred_element_type=jnp.float32)
        prob = jax.nn.softmax(logits, axis=-1)
        onehot = (batch_label[:, None] == jnp.arange(classes, dtype=jnp.int32)[None, :]).astype(
            jnp.float32
        )
        slope = ((prob - onehot) * member[:, None]).astype(jnp.bfloat16)
        back = jnp.dot(slope, w2_low.T, preferred_element_type=jnp.float32)
        sig = jax.nn.sigmoid(z)
        dz = (back * sig * (1.0 + z * (1.0 - sig))).astype(jnp.bfloat16)
        dz_full = lax.all_gather(dz, "col", axis=0, tiled=True)
        grad2 = jnp.dot(hidden.T, slope, preferred_element_type=jnp.float32)
        grad2 = lax.psum(grad2.astype(jnp.bfloat16), ("dom", "col"))
        grad1 = jnp.dot(batch_x, dz_full, preferred_element_type=jnp.float32)
        grad1 = lax.psum(grad1.astype(jnp.bfloat16), "dom")
        w1_master = w1_master - step_rate * grad1.astype(jnp.float32)
        w2_master = w2_master - step_rate * grad2.astype(jnp.float32)
    own = hid // ncol
    w2_new = lax.dynamic_slice_in_dim(w2_master, col * own, own, axis=0)
    return (propagated, w1_master.reshape(hops, width, hid), w2_new)


def solution(mesh):
    in_specs = (
        P("col", "dom"),
        P("dom", None, None),
        P("dom", None),
        P("dom"),
        P("dom"),
        P("dom"),
        P(None, "col", "dom"),
        P("dom"),
        P("dom", None),
        P(None, "col", None),
        P("col", None),
    )
    out_specs = (P("col", "dom"), P(None, "col", None), P("col", None))
    return jax.shard_map(
        per_device, mesh=mesh, in_specs=in_specs, out_specs=out_specs, check_vma=False
    )
```

```python
import jax
import jax.numpy as jnp
from jax import lax
from jax.sharding import PartitionSpec as P

STEPS = 2
CHUNKS = 2


step_rate = 0.02


def per_device(
    features,
    tiles,
    tile_src_part,
    tile_src_block,
    tile_dst_block,
    tile_count,
    prior_hops,
    labels,
    batch_of,
    w1,
    w2,
):
    ndom = lax.axis_size("dom")
    ncol = lax.axis_size("col")
    col = lax.axis_index("col")
    width, srows = features.shape
    tilecap, blk, _unused = tiles.shape
    sblk = srows // blk
    drows = prior_hops.shape[2]
    dblk = drows // blk
    hops = w1.shape[0]
    classes = w2.shape[1]
    hid = w1.shape[2]

    buckets = STEPS * ndom
    capm = (5 * drows + 4 * buckets - 1) // (4 * buckets)
    window = min(drows, ndom * capm)
    step_of = batch_of[:, 0] // ndom
    first = (step_of == 0).astype(jnp.int32)
    rank = jnp.cumsum(first)
    n_first = rank[drows - 1]
    index = jnp.arange(drows, dtype=jnp.int32)
    place = jnp.where(first == 1, rank - 1, n_first + index - rank)
    moves = (place[:, None] == index[None, :]).astype(jnp.bfloat16)

    moves = lax.optimization_barrier(moves)

    blocks = features.reshape(width, sblk, blk)
    piece = lax.all_gather(blocks, "dom", axis=1, tiled=True)
    wide = -(-classes // 128) * 128
    w2_own = w2.astype(jnp.float32)

    def whole_w2(own):
        low = jnp.pad(own.astype(jnp.bfloat16), ((0, 0), (0, wide - classes)))
        return lax.all_gather(low, "col", axis=0, tiled=True)[:, :classes]

    tag_row = jnp.broadcast_to(labels.astype(jnp.bfloat16)[None, :], (16, drows))
    known = jnp.concatenate(
        [features[:, :drows], prior_hops[0], prior_hops[1], tag_row], axis=0
    )
    known = jnp.dot(known, moves, preferred_element_type=jnp.float32).astype(jnp.bfloat16)
    tags = known[(hops - 1) * width].astype(jnp.int32)
    known = known[: (hops - 1) * width]

    valid = (jnp.arange(tilecap, dtype=jnp.int32) < tile_count[0]).astype(jnp.float32)
    gblock = tile_src_part[:, 0] * sblk + tile_src_block
    sources = jnp.take(piece, gblock, axis=1, mode="clip")
    contrib = (
        jnp.einsum("dtk,tik->dti", sources, tiles, preferred_element_type=jnp.float32)
        * valid[None, :, None]
    )
    target = (tile_dst_block[:, None] == jnp.arange(dblk, dtype=jnp.int32)[None, :]).astype(
        jnp.float32
    )
    summed = jnp.einsum("dti,tb->dbi", contrib, target, precision=lax.Precision.HIGHEST)
    propagated = summed.reshape(width, drows).astype(jnp.bfloat16)
    fresh = jnp.dot(propagated, moves, preferred_element_type=jnp.float32).astype(jnp.bfloat16)

    share = window // ncol
    span = hid // CHUNKS
    w1_known = jnp.concatenate([w1[0], w1[2], w1[3]], axis=0).astype(jnp.float32)
    w1_fresh = w1[1].astype(jnp.float32)
    cuts = [slice(n * span, (n + 1) * span) for n in range(CHUNKS)]
    w1_known = [w1_known[:, cut] for cut in cuts]
    w1_fresh = [w1_fresh[:, cut] for cut in cuts]

    def rows_by(x, w):
        return jnp.einsum(
            "dr,dj->rj", x, w.astype(jnp.bfloat16), preferred_element_type=jnp.float32
        )

    def after(value, earlier):
        return value if earlier is None else lax.optimization_barrier((value, earlier))[0]

    for step in range(STEPS):
        start = 0 if step == 0 else drows - window
        x_known = lax.slice_in_dim(known, start, start + window, axis=1)
        x_fresh = lax.slice_in_dim(fresh, start, start + window, axis=1)
        spot = start + col * share + jnp.arange(share, dtype=jnp.int32)
        batch_label = lax.dynamic_slice_in_dim(tags, start + col * share, share)
        member = (spot < n_first) if step == 0 else (spot >= n_first)
        member = member.astype(jnp.float32)
        w2_low = whole_w2(w2_own)
        sums, last = [], None
        for n in range(CHUNKS):
            term = rows_by(x_known, w1_known[n]) + rows_by(x_fresh, w1_fresh[n])
            term = after(term.astype(jnp.bfloat16), last)
            last = lax.psum_scatter(term, "col", scatter_dimension=0, tiled=True)
            sums.append(last)
        z = jnp.concatenate(sums, axis=1).astype(jnp.float32)
        hidden = jax.nn.silu(z).astype(jnp.bfloat16)
        logits = jnp.dot(hidden, w2_low, preferred_element_type=jnp.float32)
        prob = jax.nn.softmax(logits, axis=-1)
        onehot = (batch_label[:, None] == jnp.arange(classes, dtype=jnp.int32)[None, :]).astype(
            jnp.float32
        )
        slope = ((prob - onehot) * member[:, None]).astype(jnp.bfloat16)
        back = jnp.dot(slope, w2_low.T, preferred_element_type=jnp.float32)
        sig = jax.nn.sigmoid(z)
        dz = (back * sig * (1.0 + z * (1.0 - sig))).astype(jnp.bfloat16)
        grad2 = jnp.dot(hidden.T, slope, preferred_element_type=jnp.float32)
        grad2 = jnp.pad(grad2.astype(jnp.bfloat16), ((0, 0), (0, wide - classes)))
        grad2 = lax.psum_scatter(grad2, "col", scatter_dimension=0, tiled=True)
        last, last_sum = None, None
        for n in range(CHUNKS):
            last = lax.all_gather(after(dz[:, cuts[n]], last), "col", axis=0, tiled=True)
            both = jnp.concatenate(
                [
                    jnp.dot(x, last, preferred_element_type=jnp.float32).astype(jnp.bfloat16)
                    for x in (x_known, x_fresh)
                ],
                axis=0,
            )
            both = after(both, last_sum)
            if n == CHUNKS - 1:
                both, grad2 = lax.psum((both, grad2), "dom")
            else:
                both = lax.psum(both, "dom")
            last_sum = both
            both = both.astype(jnp.float32)
            w1_known[n] = w1_known[n] - step_rate * both[: (hops - 1) * width]
            w1_fresh[n] = w1_fresh[n] - step_rate * both[(hops - 1) * width :]
        w2_own = w2_own - step_rate * grad2[:, :classes].astype(jnp.float32)
    w1_known = jnp.concatenate(w1_known, axis=1).reshape(hops - 1, width, hid)
    w1_fresh = jnp.concatenate(w1_fresh, axis=1)[None]
    w1_new = jnp.concatenate([w1_known[:1], w1_fresh, w1_known[1:]], axis=0)
    return (propagated, w1_new, w2_own)


def solution(mesh):
    in_specs = (
        P("col", "dom"),
        P("dom", None, None),
        P("dom", None),
        P("dom"),
        P("dom"),
        P("dom"),
        P(None, "col", "dom"),
        P("dom"),
        P("dom", None),
        P(None, "col", None),
        P("col", None),
    )
    out_specs = (P("col", "dom"), P(None, "col", None), P("col", None))
    return jax.shard_map(
        per_device, mesh=mesh, in_specs=in_specs, out_specs=out_specs, check_vma=False
    )
```

```python
import jax
import jax.numpy as jnp
from jax import lax
from jax.sharding import PartitionSpec as P

STEPS = 2
CHUNKS = 1


step_rate = 0.02


def per_device(
    features,
    tiles,
    tile_src_part,
    tile_src_block,
    tile_dst_block,
    tile_count,
    prior_hops,
    labels,
    batch_of,
    w1,
    w2,
):
    ndom = lax.axis_size("dom")
    ncol = lax.axis_size("col")
    col = lax.axis_index("col")
    width, srows = features.shape
    tilecap, blk, _unused = tiles.shape
    sblk = srows // blk
    drows = prior_hops.shape[2]
    dblk = drows // blk
    hops = w1.shape[0]
    classes = w2.shape[1]
    hid = w1.shape[2]

    buckets = STEPS * ndom
    capm = (5 * drows + 4 * buckets - 1) // (4 * buckets)
    window = min(drows, ndom * capm)
    step_of = batch_of[:, 0] // ndom
    first = (step_of == 0).astype(jnp.int32)
    rank = jnp.cumsum(first)
    n_first = rank[drows - 1]
    index = jnp.arange(drows, dtype=jnp.int32)
    place = jnp.where(first == 1, rank - 1, n_first + index - rank)
    moves = (place[:, None] == index[None, :]).astype(jnp.bfloat16)

    moves = lax.optimization_barrier(moves)

    blocks = features.reshape(width, sblk, blk)
    piece = lax.all_gather(blocks, "dom", axis=1, tiled=True)
    wide = -(-classes // 128) * 128
    w2_own = w2.astype(jnp.float32)

    def whole_w2(own):
        low = jnp.pad(own.astype(jnp.bfloat16), ((0, 0), (0, wide - classes)))
        return lax.all_gather(low, "col", axis=0, tiled=True)[:, :classes]

    tag_row = jnp.broadcast_to(labels.astype(jnp.bfloat16)[None, :], (16, drows))
    known = jnp.concatenate(
        [features[:, :drows], prior_hops[0], prior_hops[1], tag_row], axis=0
    )
    known = jnp.dot(known, moves, preferred_element_type=jnp.float32).astype(jnp.bfloat16)
    tags = known[(hops - 1) * width].astype(jnp.int32)
    known = known[: (hops - 1) * width]

    valid = (jnp.arange(tilecap, dtype=jnp.int32) < tile_count[0]).astype(jnp.float32)
    gblock = tile_src_part[:, 0] * sblk + tile_src_block
    sources = jnp.take(piece, gblock, axis=1, mode="clip")
    contrib = (
        jnp.einsum("dtk,tik->dti", sources, tiles, preferred_element_type=jnp.float32)
        * valid[None, :, None]
    )
    target = (tile_dst_block[:, None] == jnp.arange(dblk, dtype=jnp.int32)[None, :]).astype(
        jnp.float32
    )
    summed = jnp.einsum("dti,tb->dbi", contrib, target, precision=lax.Precision.HIGHEST)
    propagated = summed.reshape(width, drows).astype(jnp.bfloat16)
    fresh = jnp.dot(propagated, moves, preferred_element_type=jnp.float32).astype(jnp.bfloat16)

    share = window // ncol
    span = hid // CHUNKS
    w1_known = jnp.concatenate([w1[0], w1[2], w1[3]], axis=0).astype(jnp.float32)
    w1_fresh = w1[1].astype(jnp.float32)
    cuts = [slice(n * span, (n + 1) * span) for n in range(CHUNKS)]
    w1_known = [w1_known[:, cut] for cut in cuts]
    w1_fresh = [w1_fresh[:, cut] for cut in cuts]

    def rows_by(x, w):
        return jnp.einsum(
            "dr,dj->rj", x, w.astype(jnp.bfloat16), preferred_element_type=jnp.float32
        )

    def after(value, earlier):
        return value if earlier is None else lax.optimization_barrier((value, earlier))[0]

    for step in range(STEPS):
        start = 0 if step == 0 else drows - window
        x_known = lax.slice_in_dim(known, start, start + window, axis=1)
        x_fresh = lax.slice_in_dim(fresh, start, start + window, axis=1)
        spot = start + col * share + jnp.arange(share, dtype=jnp.int32)
        batch_label = lax.dynamic_slice_in_dim(tags, start + col * share, share)
        member = (spot < n_first) if step == 0 else (spot >= n_first)
        member = member.astype(jnp.float32)
        w2_low = whole_w2(w2_own)
        sums, last = [], None
        for n in range(CHUNKS):
            term = rows_by(x_known, w1_known[n]) + rows_by(x_fresh, w1_fresh[n])
            term = after(term.astype(jnp.bfloat16), last)
            last = lax.psum_scatter(term, "col", scatter_dimension=0, tiled=True)
            sums.append(last)
        z = jnp.concatenate(sums, axis=1).astype(jnp.float32)
        hidden = jax.nn.silu(z).astype(jnp.bfloat16)
        logits = jnp.dot(hidden, w2_low, preferred_element_type=jnp.float32)
        prob = jax.nn.softmax(logits, axis=-1)
        onehot = (batch_label[:, None] == jnp.arange(classes, dtype=jnp.int32)[None, :]).astype(
            jnp.float32
        )
        slope = ((prob - onehot) * member[:, None]).astype(jnp.bfloat16)
        back = jnp.dot(slope, w2_low.T, preferred_element_type=jnp.float32)
        sig = jax.nn.sigmoid(z)
        dz = (back * sig * (1.0 + z * (1.0 - sig))).astype(jnp.bfloat16)
        grad2 = jnp.dot(hidden.T, slope, preferred_element_type=jnp.float32)
        grad2 = jnp.pad(grad2.astype(jnp.bfloat16), ((0, 0), (0, wide - classes)))
        grad2 = lax.psum_scatter(grad2, "col", scatter_dimension=0, tiled=True)
        last, last_sum = None, None
        for n in range(CHUNKS):
            last = lax.all_gather(after(dz[:, cuts[n]], last), "col", axis=0, tiled=True)
            both = jnp.concatenate(
                [
                    jnp.dot(x, last, preferred_element_type=jnp.float32).astype(jnp.bfloat16)
                    for x in (x_known, x_fresh)
                ],
                axis=0,
            )
            both = after(both, last_sum)
            if n == CHUNKS - 1:
                both, grad2 = lax.psum((both, grad2), "dom")
            else:
                both = lax.psum(both, "dom")
            last_sum = both
            both = both.astype(jnp.float32)
            w1_known[n] = w1_known[n] - step_rate * both[: (hops - 1) * width]
            w1_fresh[n] = w1_fresh[n] - step_rate * both[(hops - 1) * width :]
        w2_own = w2_own - step_rate * grad2[:, :classes].astype(jnp.float32)
    w1_known = jnp.concatenate(w1_known, axis=1).reshape(hops - 1, width, hid)
    w1_fresh = jnp.concatenate(w1_fresh, axis=1)[None]
    w1_new = jnp.concatenate([w1_known[:1], w1_fresh, w1_known[1:]], axis=0)
    return (propagated, w1_new, w2_own)


def solution(mesh):
    in_specs = (
        P("col", "dom"),
        P("dom", None, None),
        P("dom", None),
        P("dom"),
        P("dom"),
        P("dom"),
        P(None, "col", "dom"),
        P("dom"),
        P("dom", None),
        P(None, "col", None),
        P("col", None),
    )
    out_specs = (P("col", "dom"), P(None, "col", None), P("col", None))
    return jax.shard_map(
        per_device, mesh=mesh, in_specs=in_specs, out_specs=out_specs, check_vma=False
    )
```

```python
import jax
import jax.numpy as jnp
from jax import lax
from jax.sharding import PartitionSpec as P

STEPS = 2
CHUNKS = 1


step_rate = 0.02


def per_device(
    features,
    tiles,
    tile_src_part,
    tile_src_block,
    tile_dst_block,
    tile_count,
    prior_hops,
    labels,
    batch_of,
    w1,
    w2,
):
    ndom = lax.axis_size("dom")
    ncol = lax.axis_size("col")
    col = lax.axis_index("col")
    width, srows = features.shape
    tilecap, blk, _unused = tiles.shape
    sblk = srows // blk
    drows = prior_hops.shape[2]
    dblk = drows // blk
    hops = w1.shape[0]
    classes = w2.shape[1]
    hid = w1.shape[2]

    buckets = STEPS * ndom
    capm = (5 * drows + 4 * buckets - 1) // (4 * buckets)
    window = min(drows, ndom * capm)
    step_of = batch_of[:, 0] // ndom
    first = (step_of == 0).astype(jnp.int32)
    rank = jnp.cumsum(first)
    n_first = rank[drows - 1]
    index = jnp.arange(drows, dtype=jnp.int32)
    place = jnp.where(first == 1, rank - 1, n_first + index - rank)
    moves = (place[:, None] == index[None, :]).astype(jnp.bfloat16)

    moves = lax.optimization_barrier(moves)

    blocks = features.reshape(width, sblk, blk)
    piece = lax.all_gather(blocks, "dom", axis=1, tiled=True)
    wide = -(-classes // 128) * 128
    w2_own = w2.astype(jnp.float32)

    def whole_w2(own):
        low = jnp.pad(own.astype(jnp.bfloat16), ((0, 0), (0, wide - classes)))
        return lax.all_gather(low, "col", axis=0, tiled=True)[:, :classes]

    tag_row = jnp.broadcast_to(labels.astype(jnp.bfloat16)[None, :], (16, drows))
    known = jnp.concatenate(
        [features[:, :drows], prior_hops[0], prior_hops[1], tag_row], axis=0
    )
    known = jnp.dot(known, moves, preferred_element_type=jnp.float32).astype(jnp.bfloat16)
    tags = known[(hops - 1) * width].astype(jnp.int32)
    known = known[: (hops - 1) * width]

    valid = (jnp.arange(tilecap, dtype=jnp.int32) < tile_count[0]).astype(jnp.float32)
    gblock = tile_src_part[:, 0] * sblk + tile_src_block
    sources = jnp.take(piece, gblock, axis=1, mode="clip")
    contrib = (
        jnp.einsum("dtk,tik->dti", sources, tiles, preferred_element_type=jnp.float32)
        * valid[None, :, None]
    )
    target = (tile_dst_block[:, None] == jnp.arange(dblk, dtype=jnp.int32)[None, :]).astype(
        jnp.float32
    )
    summed = jnp.einsum("dti,tb->dbi", contrib, target, precision=lax.Precision.HIGHEST)
    propagated = summed.reshape(width, drows).astype(jnp.bfloat16)
    fresh = jnp.dot(propagated, moves, preferred_element_type=jnp.float32).astype(jnp.bfloat16)

    share = window // ncol
    span = hid // CHUNKS
    w1_known = jnp.concatenate([w1[0], w1[2], w1[3]], axis=0).astype(jnp.float32)
    w1_fresh = w1[1].astype(jnp.float32)
    cuts = [slice(n * span, (n + 1) * span) for n in range(CHUNKS)]
    w1_known = [w1_known[:, cut] for cut in cuts]
    w1_fresh = [w1_fresh[:, cut] for cut in cuts]

    def rows_by(x, w):
        return jnp.einsum(
            "dr,dj->rj", x, w.astype(jnp.bfloat16), preferred_element_type=jnp.float32
        )

    def after(value, earlier):
        return value if earlier is None else lax.optimization_barrier((value, earlier))[0]

    for step in range(STEPS):
        start = 0 if step == 0 else drows - window
        x_known = lax.slice_in_dim(known, start, start + window, axis=1)
        x_fresh = lax.slice_in_dim(fresh, start, start + window, axis=1)
        spot = start + col * share + jnp.arange(share, dtype=jnp.int32)
        batch_label = lax.dynamic_slice_in_dim(tags, start + col * share, share)
        member = (spot < n_first) if step == 0 else (spot >= n_first)
        member = member.astype(jnp.float32)
        w2_low = whole_w2(w2_own)
        sums, last = [], None
        for n in range(CHUNKS):
            term = rows_by(x_known, w1_known[n]) + rows_by(x_fresh, w1_fresh[n])
            term = after(term.astype(jnp.bfloat16), last)
            last = lax.psum_scatter(term, "col", scatter_dimension=0, tiled=True)
            sums.append(last)
        z = jnp.concatenate(sums, axis=1).astype(jnp.float32)
        hidden = jax.nn.silu(z).astype(jnp.bfloat16)
        logits = jnp.dot(hidden, w2_low, preferred_element_type=jnp.float32)
        prob = jax.nn.softmax(logits, axis=-1)
        onehot = (batch_label[:, None] == jnp.arange(classes, dtype=jnp.int32)[None, :]).astype(
            jnp.float32
        )
        slope = ((prob - onehot) * member[:, None]).astype(jnp.bfloat16)
        back = jnp.dot(slope, w2_low.T, preferred_element_type=jnp.float32)
        sig = jax.nn.sigmoid(z)
        dz = (back * sig * (1.0 + z * (1.0 - sig))).astype(jnp.bfloat16)
        grad2 = jnp.dot(hidden.T, slope, preferred_element_type=jnp.float32)
        grad2 = jnp.pad(grad2.astype(jnp.bfloat16), ((0, 0), (0, wide - classes)))
        own = hid // ncol
        parts = []
        for k in range(ncol):
            part = lax.dynamic_slice_in_dim(grad2, (col + k) % ncol * own, own, axis=0)
            if k:
                part = lax.ppermute(part, "col", [(c, (c + k) % ncol) for c in range(ncol)])
            parts.append(part.astype(jnp.float32))
        grad2 = sum(parts).astype(jnp.bfloat16)
        last, last_sum = None, None
        for n in range(CHUNKS):
            last = lax.all_gather(after(dz[:, cuts[n]], last), "col", axis=0, tiled=True)
            both = jnp.concatenate(
                [
                    jnp.dot(x, last, preferred_element_type=jnp.float32).astype(jnp.bfloat16)
                    for x in (x_known, x_fresh)
                ],
                axis=0,
            )
            both = after(both, last_sum)
            if n == CHUNKS - 1:
                both, grad2 = lax.psum((both, grad2), "dom")
            else:
                both = lax.psum(both, "dom")
            last_sum = both
            both = both.astype(jnp.float32)
            w1_known[n] = w1_known[n] - step_rate * both[: (hops - 1) * width]
            w1_fresh[n] = w1_fresh[n] - step_rate * both[(hops - 1) * width :]
        w2_own = w2_own - step_rate * grad2[:, :classes].astype(jnp.float32)
    w1_known = jnp.concatenate(w1_known, axis=1).reshape(hops - 1, width, hid)
    w1_fresh = jnp.concatenate(w1_fresh, axis=1)[None]
    w1_new = jnp.concatenate([w1_known[:1], w1_fresh, w1_known[1:]], axis=0)
    return (propagated, w1_new, w2_own)


def solution(mesh):
    in_specs = (
        P("col", "dom"),
        P("dom", None, None),
        P("dom", None),
        P("dom"),
        P("dom"),
        P("dom"),
        P(None, "col", "dom"),
        P("dom"),
        P("dom", None),
        P(None, "col", None),
        P("col", None),
    )
    out_specs = (P("col", "dom"), P(None, "col", None), P("col", None))
    return jax.shard_map(
        per_device, mesh=mesh, in_specs=in_specs, out_specs=out_specs, check_vma=False
    )
```
